32 devices in a mesh: seg: 8 (over z, x), tok: 4 (over y, core).
Axes of the slice: x: 2, y: 2, z: 4, core: 2. Of those that a mesh axis runs over, the one named last changes fastest.
Arguments:
- queries: bfloat16 [8192, 2048], P(('seg', 'tok')), may hold values from -40 to 40
- keys: bfloat16 [8192, 512], P(('seg', 'tok')), may hold values from -40 to 40
- values: bfloat16 [8192, 512], P(('seg', 'tok')), may hold values from -6 to 6
- gain_mem: float32 [2048], replicated, may hold values from 0.25 to 1.75
- gain_dot: float32 [2048], replicated, may hold values from 0.25 to 1.75
- out_weight: bfloat16 [2048, 2048], replicated, may hold values from -0.125 to 0.125
Outputs:
- layer_out: bfloat16 [8192, 2048], P(('seg', 'tok'))
The draws below stay inside these ranges and needn't reach their ends.
All inputs are finite; a program needn't handle non-finite values.
Results may differ from the reference program's by a relative error of at most 0.008.
Values may be sent and summed in bfloat16 or wider, within the bound.
A program may use at most 128 MiB of HBM per device.

```python
import jax
import jax.numpy as jnp
from jax import lax

QUERY_HEADS = 16
KEY_VALUE_HEADS = 4
HEAD_DIMENSION = 128
D = 2048
SEGMENT_TOKENS = 1024
TOTAL_TOKENS = 8192


def draw_keys(key, part):
    random_sample = jax.random.truncated_normal(jax.random.fold_in(key, 3), -6.0, 6.0, (TOTAL_TOKENS, KEY_VALUE_HEADS * HEAD_DIMENSION), jnp.float32)
    return random_sample.astype(jnp.bfloat16)


def draw_queries(key, part):
    random_sample = jax.random.truncated_normal(jax.random.fold_in(key, 4), -6.0, 6.0, (TOTAL_TOKENS, QUERY_HEADS * HEAD_DIMENSION), jnp.float32)
    return random_sample.astype(jnp.bfloat16)


def shard_levels(key, dims, split, low, high):
    def one(position, shards_of):
        steps = jax.random.uniform(jax.random.fold_in(jax.random.fold_in(key, 6), position), (shards_of,), jnp.float32, low / len(split), high / len(split))
        return jnp.repeat(jnp.exp(steps), dims[position] // shards_of).reshape((-1,) + (1,) * (len(dims) - position - 1))

    level = one(*split[0])
    for cut in split[1:]:
        level = level * one(*cut)
    return level


def centred(key, dims, width, limit, pieces=(), kind=jnp.bfloat16):
    array = width * jax.random.normal(key, dims, jnp.float32)
    if pieces:
        array = array * shard_levels(key, dims, pieces, -0.22, 0.18)
    return jnp.clip(array, -limit, limit).astype(kind)


def setup_inputs(seed: int = 0) -> dict:
    arg_keys = jax.random.split(jax.random.key(seed), 7)
    queries = draw_queries(jax.random.fold_in(arg_keys[6], 71), 0)
    keys = draw_keys(jax.random.fold_in(arg_keys[6], 71), 0)
    values = centred(arg_keys[2], (TOTAL_TOKENS, KEY_VALUE_HEADS * HEAD_DIMENSION), 1.0, 6.0, ((0, 32),))
    gain_mem = jnp.clip(1.0 + 0.15 * jax.random.normal(arg_keys[3], (D,), jnp.float32), 0.25, 1.75)
    gain_dot = jnp.clip(1.0 + 0.15 * jax.random.normal(arg_keys[4], (D,), jnp.float32), 0.25, 1.75)
    out_weight = centred(arg_keys[5], (D, D), D ** -0.5, 0.125)
    return {"queries": queries, "keys": keys, "values": values, "gain_mem": gain_mem, "gain_dot": gain_dot, "out_weight": out_weight}


def feature_map(inputs):
    return jax.nn.elu(inputs) + 1.0

def head_norm(inputs, gain):
    return inputs * lax.rsqrt(lax.optimization_barrier(jnp.mean(inputs * inputs, axis=-1, keepdims=True)) + 1e-06) * gain

def reference(queries, keys, values, gain_mem, gain_dot, out_weight):
    number_of_segments = TOTAL_TOKENS // SEGMENT_TOKENS
    query_group_width = QUERY_HEADS // KEY_VALUE_HEADS
    highest = lax.Precision.HIGHEST
    segment_key_tiles = keys.reshape(number_of_segments, SEGMENT_TOKENS, KEY_VALUE_HEADS, HEAD_DIMENSION)
    segment_value_tiles = values.reshape(number_of_segments, SEGMENT_TOKENS, KEY_VALUE_HEADS, HEAD_DIMENSION)
    sig_keys = feature_map(segment_key_tiles.astype(jnp.float32)).astype(jnp.bfloat16)
    parts = jnp.einsum('sthd,sthe->shde', sig_keys.astype(jnp.float32), segment_value_tiles.astype(jnp.float32), precision=highest)
    running = jnp.cumsum(parts, axis=0)
    earlier = jnp.concatenate([jnp.zeros_like(parts[:1]), running[:-1]], axis=0)
    segment_query_tiles = queries.reshape(number_of_segments, SEGMENT_TOKENS, KEY_VALUE_HEADS, query_group_width, HEAD_DIMENSION)
    gain_memory = gain_mem.reshape(QUERY_HEADS, HEAD_DIMENSION)
    gain_attend = gain_dot.reshape(QUERY_HEADS, HEAD_DIMENSION)
    positions = jnp.arange(SEGMENT_TOKENS, dtype=jnp.int32)
    causal = positions[:, None] >= positions[None, :]
    scale = float(HEAD_DIMENSION) ** (-0.5)

    def per_segment(segment_items):
        query_block, key_block, value_block, memory = segment_items
        scores = jnp.einsum('rgjd,cgd->gjrc', query_block.astype(jnp.float32), key_block.astype(jnp.float32), precision=highest) * scale
        scores = jnp.where(causal, scores, -jnp.inf)
        row_max = lax.optimization_barrier(jnp.max(scores, axis=-1, keepdims=True))
        weights = jnp.where(causal, jnp.exp(scores - row_max), 0.0)
        denominator = lax.optimization_barrier(jnp.sum(weights, axis=-1, keepdims=True))
        weighted = jnp.einsum('gjrc,cgd->gjrd', weights.astype(jnp.bfloat16).astype(jnp.float32), value_block.astype(jnp.float32), precision=highest)
        dot_part = jnp.transpose(weighted / denominator, (2, 0, 1, 3)).reshape(SEGMENT_TOKENS, QUERY_HEADS, HEAD_DIMENSION)
        sig_queries = feature_map(query_block.astype(jnp.float32))
        memory_part = jnp.einsum('rgjd,gde->rgje', sig_queries, memory, precision=highest).reshape(SEGMENT_TOKENS, QUERY_HEADS, HEAD_DIMENSION)
        mixed = (0.5 * (head_norm(memory_part, gain_memory) + head_norm(dot_part, gain_attend))).astype(jnp.bfloat16)
        mixed = mixed.reshape(SEGMENT_TOKENS, QUERY_HEADS * HEAD_DIMENSION)
        return jnp.dot(mixed, out_weight, preferred_element_type=jnp.float32).astype(jnp.bfloat16)
    outputs = lax.map(per_segment, (segment_query_tiles, segment_key_tiles, segment_value_tiles, earlier))
    return outputs.reshape(TOTAL_TOKENS, QUERY_HEADS * HEAD_DIMENSION)
```

```python
import functools

import jax
import jax.numpy as jnp
from jax import lax
from jax.experimental import pallas as pl
from jax.experimental.pallas import tpu as pltpu
from jax.sharding import PartitionSpec as P

HEAD = 128
MESH = pl.DeviceIdType.MESH
LOG2E = 1.4426950408889634


def feature_map(x):
    return jnp.where(x > 0.0, x + 1.0, jnp.exp(x))


def norm(x, gain):
    return x * lax.rsqrt(jnp.mean(x * x, axis=-1, keepdims=True) + 1e-06) * gain


def kernel(
    n_seg, n_tok, groups, per_group,
    q_ref, k_ref, v_ref, gain_mem_ref, gain_dot_ref, mixed_ref,
    kv, parts, terms, own, earlier, memory, dots,
    kv_recv, far_send, mate_send, part_send, part_recv,
    own_send, earlier_recv, memory_send, memory_recv,
):
    seg = lax.axis_index("seg")
    tok = lax.axis_index("tok")
    rows = q_ref.shape[0]
    share = HEAD // n_tok
    cores = 2 if n_tok % 2 == 0 else 1
    chips = n_tok // cores
    core = lax.rem(tok, cores)
    mate = tok + 1 - 2 * core if cores == 2 else tok

    barrier = pltpu.get_barrier_semaphore()
    for step in range(1, n_tok):
        pl.semaphore_signal(
            barrier, inc=1, device_id={"tok": lax.rem(tok + step, n_tok)}, device_id_type=MESH
        )

    def greet(step, carry):
        pl.semaphore_signal(
            barrier, inc=1, device_id={"seg": lax.rem(seg + step, n_seg)}, device_id_type=MESH
        )
        return carry

    lax.fori_loop(1, n_seg, greet, 0)

    for g in range(groups):
        columns = slice(g * HEAD, (g + 1) * HEAD)
        key, value = k_ref[:, columns], v_ref[:, columns]
        kv[tok, g, 0] = key
        kv[tok, g, 1] = value
        sig = feature_map(key.astype(jnp.float32)).astype(jnp.bfloat16)
        part = lax.dot_general(
            sig, value, (((0,), (0,)), ((), ())), preferred_element_type=jnp.float32
        )
        parts[:, g] = part.astype(jnp.bfloat16).reshape(n_tok, share, HEAD)
    pl.semaphore_wait(barrier, n_tok - 1 + n_seg - 1)

    def remote(src, dst, send, recv, device):
        return pltpu.make_async_remote_copy(
            src_ref=src, dst_ref=dst, send_sem=send, recv_sem=recv,
            device_id=device, device_id_type=MESH,
        )

    def part_copy(step):
        peer = lax.rem(tok + step, n_tok)
        return remote(
            parts.at[peer], terms.at[tok], part_send.at[step], part_recv.at[step], {"tok": peer}
        )

    def part_arrival(step):
        source = lax.rem(tok + n_tok - step, n_tok)
        return remote(
            parts.at[source], terms.at[source], part_send.at[step], part_recv.at[step],
            {"tok": source},
        )

    def own_copy(peer):
        return remote(
            own, earlier.at[seg], own_send.at[peer], earlier_recv.at[seg], {"seg": peer}
        )

    def own_arrival(source):
        return remote(
            own, earlier.at[source], own_send.at[source], earlier_recv.at[source],
            {"seg": source},
        )

    def memory_copy(step):
        peer = lax.rem(tok + step, n_tok)
        return remote(
            memory.at[tok], memory.at[tok], memory_send.at[step], memory_recv.at[step],
            {"tok": peer},
        )

    def memory_arrival(step):
        source = lax.rem(tok + n_tok - step, n_tok)
        return remote(
            memory.at[source], memory.at[source], memory_send.at[step], memory_recv.at[step],
            {"tok": source},
        )

    def far_copy(hop, g):
        return remote(
            kv.at[tok, g], kv.at[tok, g], far_send.at[hop, g], kv_recv.at[tok, g],
            {"tok": tok + cores * hop},
        )

    def mate_copy(block, g):
        return remote(
            kv.at[block, g], kv.at[block, g], mate_send.at[block, g], kv_recv.at[block, g],
            {"tok": mate},
        )

    for step in range(1, n_tok):
        part_copy(step).start()

    def send_keys(g, carry):
        for hop in range(1, chips):
            @pl.when(tok + cores * hop < n_tok)
            def _():
                far_copy(hop, g).start()

        if cores == 2:
            @pl.when(core == 0)
            def _():
                mate_copy(tok, g).start()
        return carry

    lax.fori_loop(0, groups, send_keys, 0)

    terms[tok] = parts[tok]
    for step in range(1, n_tok):
        part_arrival(step).wait_recv()
    total = terms[0].astype(jnp.float32)
    for j in range(1, n_tok):
        total += terms[j].astype(jnp.float32)
    own[...] = total.astype(jnp.bfloat16)

    def send_own(peer, carry):
        own_copy(peer).start()
        return carry

    lax.fori_loop(seg + 1, n_seg, send_own, 0)

    def gather_earlier():
        def add(source, state):
            own_arrival(source).wait_recv()
            return state + earlier[source].astype(jnp.float32)

        state = lax.fori_loop(0, seg, add, jnp.zeros((groups, share, HEAD), jnp.float32))
        memory[tok] = state.astype(jnp.bfloat16)
        for step in range(1, n_tok):
            memory_copy(step).start()

    def forward(t, g):
        for block in range(t - cores, -1, -cores):
            mate_copy(block, g).wait_recv()
            if cores == 2:
                mate_copy(block, g).start()

    def attend(t, g):
        if cores == 2:
            for block in range(t):
                if block % 2 != t % 2:
                    mate_copy(block, g).wait_recv()
        row = lax.broadcasted_iota(jnp.int32, (rows, rows), 0)
        column = lax.broadcasted_iota(jnp.int32, (rows, rows), 1)
        ones = jnp.ones((rows, HEAD), jnp.bfloat16)
        for j in range(per_group):
            if j == per_group // 2:
                @pl.when(g + 1 < groups)
                def _():
                    forward(t, g + 1)
            columns = pl.ds(pl.multiple_of((g * per_group + j) * HEAD, HEAD), HEAD)
            query = q_ref[:, columns]
            scores = [
                lax.dot_general(
                    query, kv[b, g, 0], (((1,), (1,)), ((), ())),
                    preferred_element_type=jnp.float32,
                )
                for b in range(t + 1)
            ]
            scores[t] = jnp.where(row >= column, scores[t], -1e30)
            top = functools.reduce(jnp.maximum, scores)
            top = jnp.max(top, axis=-1, keepdims=True)
            acc = None
            for b in range(t + 1):
                weights = jnp.exp2((scores[b] - top) * (HEAD ** -0.5 * LOG2E))
                term = jnp.dot(
                    weights.astype(jnp.bfloat16),
                    jnp.concatenate([kv[b, g, 1], ones], axis=1),
                    preferred_element_type=jnp.float32,
                )
                acc = term if acc is None else acc + term
            read = acc[:, :HEAD] / acc[:, HEAD:]
            dots[:, columns] = norm(read, gain_dot_ref[:, columns])

    for t in range(n_tok):
        @pl.when(tok == t)
        def _():
            forward(t, 0)

    def group(g, carry):
        for t in range(n_tok):
            @pl.when(tok == t)
            def _():
                attend(t, g)

        @pl.when(g == 0)
        def _():
            gather_earlier()
        return carry

    lax.fori_loop(0, groups, group, 0)

    for step in range(1, n_tok):
        memory_arrival(step).wait_recv()

    def mix(g, carry):
        rows_memory = memory[:, g].reshape(HEAD, HEAD)
        for j in range(per_group):
            columns = pl.ds(pl.multiple_of((g * per_group + j) * HEAD, HEAD), HEAD)
            sig = feature_map(q_ref[:, columns].astype(jnp.float32)).astype(jnp.bfloat16)
            read = jnp.dot(sig, rows_memory, preferred_element_type=jnp.float32)
            read = norm(read, gain_mem_ref[:, columns])
            mixed_ref[:, columns] = (0.5 * (read + dots[:, columns])).astype(jnp.bfloat16)
        return carry

    lax.fori_loop(0, groups, mix, 0)

    for step in range(1, n_tok):
        part_copy(step).wait_send()
        memory_copy(step).wait_send()

    def sent_own(peer, carry):
        own_copy(peer).wait_send()
        return carry

    lax.fori_loop(seg + 1, n_seg, sent_own, 0)

    def sent_keys(g, carry):
        for hop in range(1, chips):
            @pl.when(tok + cores * hop < n_tok)
            def _():
                far_copy(hop, g).wait_send()

            if cores == 2:
                @pl.when(tok >= cores * hop)
                def _():
                    mate_copy(tok - cores * hop, g).wait_send()

        if cores == 2:
            @pl.when(core == 0)
            def _():
                mate_copy(tok, g).wait_send()
        return carry

    lax.fori_loop(0, groups, sent_keys, 0)


def local(n_seg, n_tok, queries, keys, values, gain_mem, gain_dot, out_weight):
    rows, width = queries.shape
    groups = keys.shape[1] // HEAD
    per_group = width // HEAD // groups
    share = HEAD // n_tok
    vmem = pl.BlockSpec(memory_space=pltpu.VMEM)
    dma = pltpu.SemaphoreType.DMA
    mixed = pl.pallas_call(
        functools.partial(kernel, n_seg, n_tok, groups, per_group),
        out_shape=jax.ShapeDtypeStruct((rows, width), jnp.bfloat16),
        in_specs=[vmem] * 5,
        out_specs=vmem,
        scratch_shapes=[
            pltpu.VMEM((n_tok, groups, 2, rows, HEAD), jnp.bfloat16),
            pltpu.VMEM((n_tok, groups, share, HEAD), jnp.bfloat16),
            pltpu.VMEM((n_tok, groups, share, HEAD), jnp.bfloat16),
            pltpu.VMEM((groups, share, HEAD), jnp.bfloat16),
            pltpu.VMEM((n_seg, groups, share, HEAD), jnp.bfloat16),
            pltpu.VMEM((n_tok, groups, share, HEAD), jnp.bfloat16),
            pltpu.VMEM((rows, width), jnp.float32),
            dma((n_tok, groups)),
            dma((n_tok, groups)),
            dma((n_tok, groups)),
            dma((n_tok,)),
            dma((n_tok,)),
            dma((n_seg,)),
            dma((n_seg,)),
            dma((n_tok,)),
            dma((n_tok,)),
        ],
        compiler_params=pltpu.CompilerParams(
            collective_id=0, has_side_effects=True, vmem_limit_bytes=32 * 1024 * 1024
        ),
    )(queries, keys, values, gain_mem.reshape(1, width), gain_dot.reshape(1, width))
    return jnp.dot(mixed, out_weight, preferred_element_type=jnp.float32).astype(jnp.bfloat16)


def solution(mesh):
    return jax.shard_map(
        functools.partial(local, mesh.shape["seg"], mesh.shape["tok"]),
        mesh=mesh,
        in_specs=(
            P(("seg", "tok"), None),
            P(("seg", "tok"), None),
            P(("seg", "tok"), None),
            P(),
            P(),
            P(),
        ),
        out_specs=P(("seg", "tok"), None),
        check_vma=False,
    )
```

```python
import functools

import jax
import jax.numpy as jnp
from jax import lax
from jax.experimental import pallas as pl
from jax.experimental.pallas import tpu as pltpu
from jax.sharding import PartitionSpec as P

HEAD = 128
MESH = pl.DeviceIdType.MESH
LOG2E = 1.4426950408889634


def feature_map(x):
    return jnp.where(x > 0.0, x + 1.0, jnp.exp(x))


def norm(x, gain):
    return x * lax.rsqrt(jnp.mean(x * x, axis=-1, keepdims=True) + 1e-06) * gain


def kernel(
    n_seg, n_tok, groups, per_group,
    q_hbm, k_hbm, v_hbm, gain_mem_hbm, gain_dot_hbm, weight_hbm, out_ref,
    q_ref, k_ref, v_ref, gain_mem_ref, gain_dot_ref, weight_ref, mixed_ref,
    kv, parts, terms, own, earlier, memory, dots,
    load, kv_recv, far_send, mate_send, part_send, part_recv,
    own_send, earlier_recv, memory_send, memory_recv,
):
    seg = lax.axis_index("seg")
    tok = lax.axis_index("tok")
    rows = q_hbm.shape[0]
    share = HEAD // n_tok
    cores = 2 if n_tok % 2 == 0 else 1
    chips = n_tok // cores
    core = lax.rem(tok, cores)
    mate = tok + 1 - 2 * core if cores == 2 else tok

    loads = [
        pltpu.make_async_copy(src, dst, load.at[i])
        for i, (src, dst) in enumerate((
            (k_hbm, k_ref), (v_hbm, v_ref), (q_hbm, q_ref),
            (gain_mem_hbm, gain_mem_ref), (gain_dot_hbm, gain_dot_ref),
            (weight_hbm, weight_ref),
        ))
    ]
    for copy in loads:
        copy.start()

    barrier = pltpu.get_barrier_semaphore()
    for step in range(1, n_tok):
        pl.semaphore_signal(
            barrier, inc=1, device_id={"tok": lax.rem(tok + step, n_tok)}, device_id_type=MESH
        )

    def greet(step, carry):
        pl.semaphore_signal(
            barrier, inc=1, device_id={"seg": lax.rem(seg + step, n_seg)}, device_id_type=MESH
        )
        return carry

    lax.fori_loop(1, n_seg, greet, 0)

    for copy in loads[:2]:
        copy.wait()
    for g in range(groups):
        columns = slice(g * HEAD, (g + 1) * HEAD)
        key, value = k_ref[:, columns], v_ref[:, columns]
        kv[tok, g, 0] = key
        kv[tok, g, 1] = value
        sig = feature_map(key.astype(jnp.float32)).astype(jnp.bfloat16)
        part = lax.dot_general(
            sig, value, (((0,), (0,)), ((), ())), preferred_element_type=jnp.float32
        )
        parts[:, g] = part.astype(jnp.bfloat16).reshape(n_tok, share, HEAD)
    pl.semaphore_wait(barrier, n_tok - 1 + n_seg - 1)

    def remote(src, dst, send, recv, device):
        return pltpu.make_async_remote_copy(
            src_ref=src, dst_ref=dst, send_sem=send, recv_sem=recv,
            device_id=device, device_id_type=MESH,
        )

    def part_copy(step):
        peer = lax.rem(tok + step, n_tok)
        return remote(
            parts.at[peer], terms.at[tok], part_send.at[step], part_recv.at[step], {"tok": peer}
        )

    def part_arrival(step):
        source = lax.rem(tok + n_tok - step, n_tok)
        return remote(
            parts.at[source], terms.at[source], part_send.at[step], part_recv.at[step],
            {"tok": source},
        )

    def own_copy(peer):
        return remote(
            own, earlier.at[seg], own_send.at[peer], earlier_recv.at[seg], {"seg": peer}
        )

    def own_arrival(source):
        return remote(
            own, earlier.at[source], own_send.at[source], earlier_recv.at[source],
            {"seg": source},
        )

    def memory_copy(step):
        peer = lax.rem(tok + step, n_tok)
        return remote(
            memory.at[tok], memory.at[tok], memory_send.at[step], memory_recv.at[step],
            {"tok": peer},
        )

    def memory_arrival(step):
        source = lax.rem(tok + n_tok - step, n_tok)
        return remote(
            memory.at[source], memory.at[source], memory_send.at[step], memory_recv.at[step],
            {"tok": source},
        )

    def far_copy(hop, g):
        return remote(
            kv.at[tok, g], kv.at[tok, g], far_send.at[hop, g], kv_recv.at[tok, g],
            {"tok": tok + cores * hop},
        )

    def mate_copy(block, g):
        return remote(
            kv.at[block, g], kv.at[block, g], mate_send.at[block, g], kv_recv.at[block, g],
            {"tok": mate},
        )

    for step in range(1, n_tok):
        part_copy(step).start()

    def send_keys(g, carry):
        for hop in range(1, chips):
            @pl.when(tok + cores * hop < n_tok)
            def _():
                far_copy(hop, g).start()

        if cores == 2:
            @pl.when(core == 0)
            def _():
                mate_copy(tok, g).start()
        return carry

    lax.fori_loop(0, groups, send_keys, 0)

    terms[tok] = parts[tok]
    for step in range(1, n_tok):
        part_arrival(step).wait_recv()
    total = terms[0].astype(jnp.float32)
    for j in range(1, n_tok):
        total += terms[j].astype(jnp.float32)
    own[...] = total.astype(jnp.bfloat16)

    def send_own(peer, carry):
        own_copy(peer).start()
        return carry

    lax.fori_loop(seg + 1, n_seg, send_own, 0)
    for copy in loads[2:5]:
        copy.wait()

    def gather_earlier():
        def add(source, state):
            own_arrival(source).wait_recv()
            return state + earlier[source].astype(jnp.float32)

        state = lax.fori_loop(0, seg, add, jnp.zeros((groups, share, HEAD), jnp.float32))
        memory[tok] = state.astype(jnp.bfloat16)
        for step in range(1, n_tok):
            memory_copy(step).start()

    def forward(t, g):
        for block in range(t - cores, -1, -cores):
            mate_copy(block, g).wait_recv()
            if cores == 2:
                mate_copy(block, g).start()

    def attend(t, g):
        if cores == 2:
            for block in range(t):
                if block % 2 != t % 2:
                    mate_copy(block, g).wait_recv()
        row = lax.broadcasted_iota(jnp.int32, (rows, rows), 0)
        column = lax.broadcasted_iota(jnp.int32, (rows, rows), 1)
        ones = jnp.ones((rows, HEAD), jnp.bfloat16)
        for j in range(per_group):
            if j == per_group // 2:
                @pl.when(g + 1 < groups)
                def _():
                    forward(t, g + 1)
            columns = pl.ds(pl.multiple_of((g * per_group + j) * HEAD, HEAD), HEAD)
            query = q_ref[:, columns]
            scores = [
                lax.dot_general(
                    query, kv[b, g, 0], (((1,), (1,)), ((), ())),
                    preferred_element_type=jnp.float32,
                )
                for b in range(t + 1)
            ]
            scores[t] = jnp.where(row >= column, scores[t], -1e30)
            top = functools.reduce(jnp.maximum, scores)
            top = jnp.max(top, axis=-1, keepdims=True)
            acc = None
            for b in range(t + 1):
                weights = jnp.exp2((scores[b] - top) * (HEAD ** -0.5 * LOG2E))
                term = jnp.dot(
                    weights.astype(jnp.bfloat16),
                    jnp.concatenate([kv[b, g, 1], ones], axis=1),
                    preferred_element_type=jnp.float32,
                )
                acc = term if acc is None else acc + term
            read = acc[:, :HEAD] / acc[:, HEAD:]
            dots[:, columns] = norm(read, gain_dot_ref[:, columns])

    for t in range(n_tok):
        @pl.when(tok == t)
        def _():
            forward(t, 0)

    def group(g, carry):
        for t in range(n_tok):
            @pl.when(tok == t)
            def _():
                attend(t, g)

        @pl.when(g == 0)
        def _():
            gather_earlier()
        return carry

    lax.fori_loop(0, groups, group, 0)

    for step in range(1, n_tok):
        memory_arrival(step).wait_recv()

    def mix(g, carry):
        rows_memory = memory[:, g].reshape(HEAD, HEAD)
        for j in range(per_group):
            columns = pl.ds(pl.multiple_of((g * per_group + j) * HEAD, HEAD), HEAD)
            sig = feature_map(q_ref[:, columns].astype(jnp.float32)).astype(jnp.bfloat16)
            read = jnp.dot(sig, rows_memory, preferred_element_type=jnp.float32)
            read = norm(read, gain_mem_ref[:, columns])
            mixed_ref[:, columns] = (0.5 * (read + dots[:, columns])).astype(jnp.bfloat16)
        return carry

    lax.fori_loop(0, groups, mix, 0)
    loads[5].wait()
    tile = min(256, out_ref.shape[1])

    def project(n, carry):
        columns = pl.ds(pl.multiple_of(n * tile, tile), tile)
        out_ref[:, columns] = jnp.dot(
            mixed_ref[...], weight_ref[:, columns], preferred_element_type=jnp.float32
        ).astype(jnp.bfloat16)
        return carry

    lax.fori_loop(0, out_ref.shape[1] // tile, project, 0)

    for step in range(1, n_tok):
        part_copy(step).wait_send()
        memory_copy(step).wait_send()

    def sent_own(peer, carry):
        own_copy(peer).wait_send()
        return carry

    lax.fori_loop(seg + 1, n_seg, sent_own, 0)

    def sent_keys(g, carry):
        for hop in range(1, chips):
            @pl.when(tok + cores * hop < n_tok)
            def _():
                far_copy(hop, g).wait_send()

            if cores == 2:
                @pl.when(tok >= cores * hop)
                def _():
                    mate_copy(tok - cores * hop, g).wait_send()

        if cores == 2:
            @pl.when(core == 0)
            def _():
                mate_copy(tok, g).wait_send()
        return carry

    lax.fori_loop(0, groups, sent_keys, 0)


def local(n_seg, n_tok, queries, keys, values, gain_mem, gain_dot, out_weight):
    rows, width = queries.shape
    groups = keys.shape[1] // HEAD
    per_group = width // HEAD // groups
    share = HEAD // n_tok
    vmem = pl.BlockSpec(memory_space=pltpu.VMEM)
    dma = pltpu.SemaphoreType.DMA
    hbm = pl.BlockSpec(memory_space=pltpu.HBM)
    return pl.pallas_call(
        functools.partial(kernel, n_seg, n_tok, groups, per_group),
        out_shape=jax.ShapeDtypeStruct((rows, out_weight.shape[1]), jnp.bfloat16),
        in_specs=[hbm] * 6,
        out_specs=vmem,
        scratch_shapes=[
            pltpu.VMEM(queries.shape, jnp.bfloat16),
            pltpu.VMEM(keys.shape, jnp.bfloat16),
            pltpu.VMEM(values.shape, jnp.bfloat16),
            pltpu.VMEM((1, width), jnp.float32),
            pltpu.VMEM((1, width), jnp.float32),
            pltpu.VMEM(out_weight.shape, jnp.bfloat16),
            pltpu.VMEM((rows, width), jnp.bfloat16),
            pltpu.VMEM((n_tok, groups, 2, rows, HEAD), jnp.bfloat16),
            pltpu.VMEM((n_tok, groups, share, HEAD), jnp.bfloat16),
            pltpu.VMEM((n_tok, groups, share, HEAD), jnp.bfloat16),
            pltpu.VMEM((groups, share, HEAD), jnp.bfloat16),
            pltpu.VMEM((n_seg, groups, share, HEAD), jnp.bfloat16),
            pltpu.VMEM((n_tok, groups, share, HEAD), jnp.bfloat16),
            pltpu.VMEM((rows, width), jnp.float32),
            dma((6,)),
            dma((n_tok, groups)),
            dma((n_tok, groups)),
            dma((n_tok, groups)),
            dma((n_tok,)),
            dma((n_tok,)),
            dma((n_seg,)),
            dma((n_seg,)),
            dma((n_tok,)),
            dma((n_tok,)),
        ],
        compiler_params=pltpu.CompilerParams(
            collective_id=0, has_side_effects=True, vmem_limit_bytes=62 * 1024 * 1024
        ),
    )(queries, keys, values, gain_mem.reshape(1, width), gain_dot.reshape(1, width), out_weight)


def solution(mesh):
    return jax.shard_map(
        functools.partial(local, mesh.shape["seg"], mesh.shape["tok"]),
        mesh=mesh,
        in_specs=(
            P(("seg", "tok"), None),
            P(("seg", "tok"), None),
            P(("seg", "tok"), None),
            P(),
            P(),
            P(),
        ),
        out_specs=P(("seg", "tok"), None),
        check_vma=False,
    )
```

```python
import functools

import jax
import jax.numpy as jnp
from jax import lax
from jax.experimental import pallas as pl
from jax.experimental.pallas import tpu as pltpu
from jax.sharding import PartitionSpec as P

HEAD = 128
MESH = pl.DeviceIdType.MESH
LOG2E = 1.4426950408889634


def feature_map(x):
    return jnp.where(x > 0.0, x + 1.0, jnp.exp(x))


def norm(x, gain):
    return x * lax.rsqrt(jnp.mean(x * x, axis=-1, keepdims=True) + 1e-06) * gain


def kernel(
    n_seg, n_tok, groups, per_group,
    q_hbm, k_hbm, v_hbm, gain_mem_hbm, gain_dot_hbm, weight_hbm, out_ref,
    q_ref, k_ref, v_ref, gain_mem_ref, gain_dot_ref, weight_ref, mixed_ref,
    kv, parts, terms, own, earlier, memory, dots,
    load, kv_recv, far_send, mate_send, part_send, part_recv,
    own_send, earlier_recv, memory_send, memory_recv,
):
    seg = lax.axis_index("seg")
    tok = lax.axis_index("tok")
    rows = q_hbm.shape[0]
    share = HEAD // n_tok
    cores = 2 if n_tok % 2 == 0 else 1
    chips = n_tok // cores
    core = lax.rem(tok, cores)
    mate = tok + 1 - 2 * core if cores == 2 else tok

    loads = [
        pltpu.make_async_copy(src, dst, load.at[i])
        for i, (src, dst) in enumerate((
            (k_hbm, k_ref), (v_hbm, v_ref), (q_hbm, q_ref),
            (gain_mem_hbm, gain_mem_ref), (gain_dot_hbm, gain_dot_ref),
            (weight_hbm, weight_ref),
        ))
    ]
    for copy in loads:
        copy.start()

    barrier = pltpu.get_barrier_semaphore()
    for step in range(1, n_tok):
        pl.semaphore_signal(
            barrier, inc=1, device_id={"tok": lax.rem(tok + step, n_tok)}, device_id_type=MESH
        )

    def greet(step, carry):
        pl.semaphore_signal(
            barrier, inc=1, device_id={"seg": lax.rem(seg + step, n_seg)}, device_id_type=MESH
        )
        return carry

    lax.fori_loop(1, n_seg, greet, 0)

    for copy in loads[:2]:
        copy.wait()
    for g in range(groups):
        columns = slice(g * HEAD, (g + 1) * HEAD)
        key, value = k_ref[:, columns], v_ref[:, columns]
        kv[tok, g, 0] = key
        kv[tok, g, 1] = value
        sig = feature_map(key.astype(jnp.float32)).astype(jnp.bfloat16)
        part = lax.dot_general(
            sig, value, (((0,), (0,)), ((), ())), preferred_element_type=jnp.float32
        )
        parts[:, g] = part.astype(jnp.bfloat16).reshape(n_tok, share, HEAD)
    pl.semaphore_wait(barrier, n_tok - 1 + n_seg - 1)

    def remote(src, dst, send, recv, device):
        return pltpu.make_async_remote_copy(
            src_ref=src, dst_ref=dst, send_sem=send, recv_sem=recv,
            device_id=device, device_id_type=MESH,
        )

    def part_copy(step):
        peer = lax.rem(tok + step, n_tok)
        return remote(
            parts.at[peer], terms.at[tok], part_send.at[step], part_recv.at[step], {"tok": peer}
        )

    def part_arrival(step):
        source = lax.rem(tok + n_tok - step, n_tok)
        return remote(
            parts.at[source], terms.at[source], part_send.at[step], part_recv.at[step],
            {"tok": source},
        )

    def own_copy(peer):
        return remote(
            own, earlier.at[seg], own_send.at[peer], earlier_recv.at[seg], {"seg": peer}
        )

    def own_arrival(source):
        return remote(
            own, earlier.at[source], own_send.at[source], earlier_recv.at[source],
            {"seg": source},
        )

    def memory_copy(step):
        peer = lax.rem(tok + step, n_tok)
        return remote(
            memory.at[tok], memory.at[tok], memory_send.at[step], memory_recv.at[step],
            {"tok": peer},
        )

    def memory_arrival(step):
        source = lax.rem(tok + n_tok - step, n_tok)
        return remote(
            memory.at[source], memory.at[source], memory_send.at[step], memory_recv.at[step],
            {"tok": source},
        )

    def far_copy(hop, g):
        return remote(
            kv.at[tok, g], kv.at[tok, g], far_send.at[hop, g], kv_recv.at[tok, g],
            {"tok": tok + cores * hop},
        )

    def mate_copy(block, g):
        return remote(
            kv.at[block, g], kv.at[block, g], mate_send.at[block, g], kv_recv.at[block, g],
            {"tok": mate},
        )

    for step in range(1, n_tok):
        part_copy(step).start()

    def send_keys(g, carry):
        for hop in range(1, chips):
            @pl.when(tok + cores * hop < n_tok)
            def _():
                far_copy(hop, g).start()

        if cores == 2:
            @pl.when(core == 0)
            def _():
                mate_copy(tok, g).start()
        return carry

    lax.fori_loop(0, groups, send_keys, 0)

    terms[tok] = parts[tok]
    for step in range(1, n_tok):
        part_arrival(step).wait_recv()
    total = terms[0].astype(jnp.float32)
    for j in range(1, n_tok):
        total += terms[j].astype(jnp.float32)
    own[...] = total.astype(jnp.bfloat16)

    def send_own(peer, carry):
        own_copy(peer).start()
        return carry

    lax.fori_loop(seg + 1, n_seg, send_own, 0)
    for copy in loads[2:5]:
        copy.wait()

    def gather_earlier():
        def add(source, state):
            own_arrival(source).wait_recv()
            return state + earlier[source].astype(jnp.float32)

        state = lax.fori_loop(0, seg, add, jnp.zeros((groups, share, HEAD), jnp.float32))
        memory[tok] = state.astype(jnp.bfloat16)
        for step in range(1, n_tok):
            memory_copy(step).start()

    def forward(t, g):
        for block in range(t - cores, -1, -cores):
            mate_copy(block, g).wait_recv()
            if cores == 2:
                mate_copy(block, g).start()

    def attend(t, g):
        if cores == 2:
            for block in range(t):
                if block % 2 != t % 2:
                    mate_copy(block, g).wait_recv()
        row = lax.broadcasted_iota(jnp.int32, (rows, rows), 0)
        column = lax.broadcasted_iota(jnp.int32, (rows, rows), 1)
        ones = jnp.ones((rows, HEAD), jnp.bfloat16)
        for j in range(per_group):
            if j == per_group // 2:
                @pl.when(g + 1 < groups)
                def _():
                    forward(t, g + 1)
            columns = pl.ds(pl.multiple_of((g * per_group + j) * HEAD, HEAD), HEAD)
            query = q_ref[:, columns]
            scores = [
                lax.dot_general(
                    query, kv[b, g, 0], (((1,), (1,)), ((), ())),
                    preferred_element_type=jnp.float32,
                )
                for b in range(t + 1)
            ]
            scores[t] = jnp.where(row >= column, scores[t], -1e30)
            top = functools.reduce(jnp.maximum, scores)
            top = jnp.max(top, axis=-1, keepdims=True)
            acc = None
            for b in range(t + 1):
                weights = jnp.exp2((scores[b] - top) * (HEAD ** -0.5 * LOG2E))
                term = jnp.dot(
                    weights.astype(jnp.bfloat16),
                    jnp.concatenate([kv[b, g, 1], ones], axis=1),
                    preferred_element_type=jnp.float32,
                )
                acc = term if acc is None else acc + term
            read = acc[:, :HEAD] / acc[:, HEAD:]
            dots[:, columns] = norm(read, gain_dot_ref[:, columns])

    for t in range(n_tok):
        @pl.when(tok == t)
        def _():
            forward(t, 0)

    def group(g, carry):
        for t in range(n_tok):
            @pl.when(tok == t)
            def _():
                attend(t, g)

        @pl.when(g == 0)
        def _():
            gather_earlier()
        return carry

    lax.fori_loop(0, groups, group, 0)

    for step in range(1, n_tok):
        memory_arrival(step).wait_recv()

    def mix(g, carry):
        rows_memory = memory[:, g].reshape(HEAD, HEAD)
        for j in range(per_group):
            columns = pl.ds(pl.multiple_of((g * per_group + j) * HEAD, HEAD), HEAD)
            sig = feature_map(q_ref[:, columns].astype(jnp.float32)).astype(jnp.bfloat16)
            read = jnp.dot(sig, rows_memory, preferred_element_type=jnp.float32)
            read = norm(read, gain_mem_ref[:, columns])
            mixed_ref[:, columns] = (0.5 * (read + dots[:, columns])).astype(jnp.bfloat16)
        return carry

    lax.fori_loop(0, groups, mix, 0, unroll=True)
    loads[5].wait()
    tile = min(512, out_ref.shape[1])

    def project(n, carry):
        columns = pl.ds(pl.multiple_of(n * tile, tile), tile)
        out_ref[:, columns] = jnp.dot(
            mixed_ref[...], weight_ref[:, columns], preferred_element_type=jnp.float32
        ).astype(jnp.bfloat16)
        return carry

    lax.fori_loop(0, out_ref.shape[1] // tile, project, 0)

    for step in range(1, n_tok):
        part_copy(step).wait_send()
        memory_copy(step).wait_send()

    def sent_own(peer, carry):
        own_copy(peer).wait_send()
        return carry

    lax.fori_loop(seg + 1, n_seg, sent_own, 0)

    def sent_keys(g, carry):
        for hop in range(1, chips):
            @pl.when(tok + cores * hop < n_tok)
            def _():
                far_copy(hop, g).wait_send()

            if cores == 2:
                @pl.when(tok >= cores * hop)
                def _():
                    mate_copy(tok - cores * hop, g).wait_send()

        if cores == 2:
            @pl.when(core == 0)
            def _():
                mate_copy(tok, g).wait_send()
        return carry

    lax.fori_loop(0, groups, sent_keys, 0)


def local(n_seg, n_tok, queries, keys, values, gain_mem, gain_dot, out_weight):
    rows, width = queries.shape
    groups = keys.shape[1] // HEAD
    per_group = width // HEAD // groups
    share = HEAD // n_tok
    vmem = pl.BlockSpec(memory_space=pltpu.VMEM)
    dma = pltpu.SemaphoreType.DMA
    hbm = pl.BlockSpec(memory_space=pltpu.HBM)
    return pl.pallas_call(
        functools.partial(kernel, n_seg, n_tok, groups, per_group),
        out_shape=jax.ShapeDtypeStruct((rows, out_weight.shape[1]), jnp.bfloat16),
        in_specs=[hbm] * 6,
        out_specs=vmem,
        scratch_shapes=[
            pltpu.VMEM(queries.shape, jnp.bfloat16),
            pltpu.VMEM(keys.shape, jnp.bfloat16),
            pltpu.VMEM(values.shape, jnp.bfloat16),
            pltpu.VMEM((1, width), jnp.float32),
            pltpu.VMEM((1, width), jnp.float32),
            pltpu.VMEM(out_weight.shape, jnp.bfloat16),
            pltpu.VMEM((rows, width), jnp.bfloat16),
            pltpu.VMEM((n_tok, groups, 2, rows, HEAD), jnp.bfloat16),
            pltpu.VMEM((n_tok, groups, share, HEAD), jnp.bfloat16),
            pltpu.VMEM((n_tok, groups, share, HEAD), jnp.bfloat16),
            pltpu.VMEM((groups, share, HEAD), jnp.bfloat16),
            pltpu.VMEM((n_seg, groups, share, HEAD), jnp.bfloat16),
            pltpu.VMEM((n_tok, groups, share, HEAD), jnp.bfloat16),
            pltpu.VMEM((rows, width), jnp.float32),
            dma((6,)),
            dma((n_tok, groups)),
            dma((n_tok, groups)),
            dma((n_tok, groups)),
            dma((n_tok,)),
            dma((n_tok,)),
            dma((n_seg,)),
            dma((n_seg,)),
            dma((n_tok,)),
            dma((n_tok,)),
        ],
        compiler_params=pltpu.CompilerParams(
            collective_id=0, has_side_effects=True, vmem_limit_bytes=62 * 1024 * 1024
        ),
    )(queries, keys, values, gain_mem.reshape(1, width), gain_dot.reshape(1, width), out_weight)


def solution(mesh):
    return jax.shard_map(
        functools.partial(local, mesh.shape["seg"], mesh.shape["tok"]),
        mesh=mesh,
        in_specs=(
            P(("seg", "tok"), None),
            P(("seg", "tok"), None),
            P(("seg", "tok"), None),
            P(),
            P(),
            P(),
        ),
        out_specs=P(("seg", "tok"), None),
        check_vma=False,
    )
```
